128 devices in a mesh: ctx: 32 (over x, y, core), grp: 4 (over z).
Axes of the slice: x: 4, y: 4, z: 4, core: 2. Of those that a mesh axis runs over, the one named last changes fastest.
Arguments:
- query: bfloat16 [32, 2, 128, 576], P('grp', None, 'ctx'), may hold values from -40 to 40
- latent_cache: bfloat16 [32, 65536, 576], P('grp', 'ctx'), may hold values from -5.5 to 5.5
- context_lengths: int32 [32], P('grp'), may hold values from 32768 to 65534, as said below
- draft_positions: int32 [32, 2], P('grp'), may hold values from 32768 to 65535, as said below
- value_up: bfloat16 [128, 512, 128], P(('ctx', 'grp')), may hold values from -1 to 1
- out_proj: bfloat16 [16384, 7168], P(('ctx', 'grp')), may hold values from -0.046875 to 0.046875
Outputs:
- attended: bfloat16 [32, 2, 7168], P('grp', None, 'ctx')
The draws below stay inside these ranges and needn't reach their ends.
Inputs may be any that keep to these rules, and one draw needn't show every extreme that they name: `context_lengths`: request 0 has 65534 committed positions and request 1 has 32768. `draft_positions`: draft slots of a request lie at or after its committed length and rise strictly along the drafts; request 0's last draft is at slot 65535 and request 1's first draft at its committed length.
All inputs are finite; a program needn't handle non-finite values.
Results may differ from the reference program's by a relative error of at most 0.03.
Values may be sent and summed in bfloat16 or wider, within the bound.
A program may use at most 128 MiB of HBM per device.

```python
import math
import jax
import jax.numpy as jnp
from jax import lax

HEADS = 128
LAT = 512
ROPE = 64
NOPE = 128
VDIM = 128
D = 7168
SPEC = 2
CTX_DEV = 2048
REQ = 32
CONTEXT = 65536
N_CTX = 32


YARN_GAIN = (0.1 * math.log(40.0) + 1.0) ** 2


def shared_anchor(key):
    anchor_rows = jnp.clip(jax.random.normal(jax.random.fold_in(key, 101), (REQ, LAT + ROPE), jnp.float32), -5.0, 5.0)
    anchor = jax.random.randint(jax.random.fold_in(key, 102), (REQ,), 0, CONTEXT // 2 - 1)
    return (anchor_rows, anchor)


def shared_direction(key):
    return jnp.clip(jax.random.normal(jax.random.fold_in(key, 301), (LAT + ROPE,), jnp.float32), -5.0, 5.0)


def shared_lengths(key):
    request_ids = jnp.arange(REQ)
    lengths = jax.random.randint(jax.random.fold_in(key, 201), (REQ,), CONTEXT // 2, CONTEXT - 1)
    lengths = jnp.where(request_ids == 0, CONTEXT - 2, jnp.where(request_ids == 1, CONTEXT // 2, lengths))
    first_slot = jax.random.randint(jax.random.fold_in(key, 202), (REQ,), lengths, CONTEXT - 1)
    first_slot = jnp.where(request_ids == 1, lengths, first_slot)
    second_slot = jax.random.randint(jax.random.fold_in(key, 203), (REQ,), first_slot + 1, CONTEXT)
    second_slot = jnp.where(request_ids == 0, CONTEXT - 1, second_slot)
    return (lengths.astype(jnp.int32), jnp.stack([first_slot, second_slot], axis=1).astype(jnp.int32))


def draw_latent_cache(key, part):
    anchor_rows, anchor = shared_anchor(key)
    direction = shared_direction(key)
    lengths, positions = shared_lengths(key)
    key = jax.random.fold_in(key, 3)
    request_ids = jnp.arange(REQ)
    values = jnp.clip(jax.random.normal(key, (REQ, CONTEXT, LAT + ROPE), jnp.float32), -5.0, 5.0)
    values = values.at[request_ids, anchor].set(anchor_rows)
    score_scale = (NOPE + ROPE) ** (-0.5) * YARN_GAIN
    lift = 18.0 / ((LAT + ROPE) * score_scale)
    pending = jnp.arange(CONTEXT)[None, :] >= lengths[:, None]
    lifted = jnp.clip(0.5 * values + lift * direction[None, None, :], -5.5, 5.5)
    values = jnp.where(pending[:, :, None], lifted, values)
    return values.astype(jnp.bfloat16)


def draw_query(key, part):
    source = key
    key = jax.random.fold_in(source, 4)
    shape = (REQ, SPEC, HEADS, LAT + ROPE)
    direction = shared_direction(source)
    adjusted = jax.random.bernoulli(jax.random.fold_in(key, 7), 0.5, (HEADS,))
    pull = jnp.where(adjusted, 0.5, 0.0)[None, None, :, None] * direction[None, None, None, :]
    values = jnp.clip(0.85 * jax.random.normal(key, shape, jnp.float32), -5.1, 5.1) + pull
    return values.astype(jnp.bfloat16)


def draw_context_lengths(key, part):
    lengths, positions = shared_lengths(key)
    return lengths


def draw_draft_positions(key, part):
    lengths, positions = shared_lengths(key)
    return positions


def level_of(stream_key, extent, pieces, least, high):
    gain, own = 1.0, jax.random.fold_in(stream_key, 6)
    for axis_at, shards_of in pieces:
        draws = jnp.exp(jax.random.uniform(jax.random.fold_in(own, axis_at), (shards_of,), jnp.float32, least / len(pieces), high / len(pieces)))
        gain = gain * jnp.repeat(draws, extent[axis_at] // shards_of).reshape([-1 if axis == axis_at else 1 for axis in range(len(extent))])
    return gain


def gaussian(stream_key, extent, spread, most, cuts=(), kind=jnp.bfloat16):
    factor_of = level_of(stream_key, extent, cuts, -0.22, 0.18) if cuts else 1.0
    result = jax.random.normal(stream_key, extent, jnp.float32) * spread * factor_of
    return jnp.minimum(jnp.maximum(result, -most), most).astype(kind)


def setup_inputs(seed: int = 0) -> dict:
    key_list = jax.random.split(jax.random.key(seed), 7)
    query = draw_query(jax.random.fold_in(key_list[6], 71), 0)
    latent_cache = draw_latent_cache(jax.random.fold_in(key_list[6], 71), 0)
    context_lengths = draw_context_lengths(jax.random.fold_in(key_list[6], 71), 0)
    draft_positions = draw_draft_positions(jax.random.fold_in(key_list[6], 71), 0)
    value_up = gaussian(key_list[4], (HEADS, LAT, VDIM), (LAT // 16) ** -0.5, 1.0, ((0, 128),))
    out_proj = gaussian(key_list[5], (HEADS * VDIM, D), (HEADS * VDIM) ** -0.5, 0.046875, ((0, 128),))
    return {"query": query, "latent_cache": latent_cache, "context_lengths": context_lengths, "draft_positions": draft_positions, "value_up": value_up, "out_proj": out_proj}


NEG_FILL = -1.0e30
YARN_GAIN = (0.1 * math.log(40.0) + 1.0) ** 2


def visible_mask(key_pos, lengths, positions):
    draft_count = positions.shape[-1]
    committed = key_pos[None, :] < lengths[:, None]
    matches = key_pos[None, None, :] == positions[:, :, None]
    draft_order = jnp.arange(draft_count, dtype=jnp.int32)
    earlier = draft_order[None, :] <= draft_order[:, None]
    drafts = jnp.any(earlier[None, :, :, None] & matches[:, None, :, :], axis=2)
    return committed[:, None, :] | drafts


def reference(query, latent_cache, context_lengths, draft_positions, value_up, out_proj):
    score_scale = (NOPE + ROPE) ** -0.5 * YARN_GAIN
    key_pos = jnp.arange(CONTEXT, dtype=jnp.int32)
    visible_all = visible_mask(key_pos, context_lengths, draft_positions)

    def attend(operands):
        query_one, cache_one, visible_one = operands
        blocks = cache_one.reshape(N_CTX, CTX_DEV, LAT + ROPE).astype(jnp.float32)
        scores = jnp.einsum("shc,bkc->shbk", query_one.astype(jnp.float32), blocks) * score_scale
        visible = visible_one.reshape(SPEC, 1, N_CTX, CTX_DEV)
        block_max = jnp.max(jnp.where(visible, scores, NEG_FILL), axis=-1)
        weights = jnp.where(visible, jnp.exp(scores - block_max[..., None]), 0.0)
        block_total = jnp.sum(weights, axis=-1)
        rounded = lax.optimization_barrier(weights.astype(jnp.bfloat16)).astype(jnp.float32)
        block_numer = jnp.einsum("shbk,bkc->shbc", rounded, blocks[:, :, :LAT])
        global_max = jnp.max(block_max, axis=-1, keepdims=True)
        factor = jnp.exp(block_max - global_max)
        denominator = jnp.sum(block_total * factor, axis=-1)
        scaled = lax.optimization_barrier((block_numer * factor[..., None]).astype(jnp.bfloat16)).astype(jnp.float32)
        numerator = jnp.sum(scaled, axis=2)
        return (numerator / denominator[..., None]).astype(jnp.bfloat16)

    latent_out = lax.map(attend, (query, latent_cache, visible_all))
    head_values = jnp.einsum("rshc,hcv->rshv", latent_out.astype(jnp.float32), value_up.astype(jnp.float32)).astype(jnp.bfloat16)
    flat_values = head_values.reshape(REQ * SPEC, HEADS * VDIM)
    attended = jnp.dot(flat_values, out_proj, preferred_element_type=jnp.float32)
    return attended.reshape(REQ, SPEC, D).astype(jnp.bfloat16)
```

```python
import math

import jax
import jax.numpy as jnp
from jax import lax
from jax.experimental import pallas as pl
from jax.experimental.pallas import tpu as pltpu
from jax.sharding import PartitionSpec as P

LAT = 512
ROPE = 64
NOPE = 128
WIDTH = LAT + ROPE
STAT = LAT + 128

YARN_GAIN = (0.1 * math.log(40.0) + 1.0) ** 2
SCALE = (NOPE + ROPE) ** -0.5 * YARN_GAIN * math.log2(math.e)
NEG_FILL = -1e30

REQ_DEV = 8
OWN = REQ_DEV // 2
KEYS = 2048
CHIPS = 16
ROWS = 16
HALF = 8 * ROWS
COLS = 896
OUT = 224
F32 = jnp.float32
BF16 = jnp.bfloat16
MESH = pl.DeviceIdType.MESH


def dot_nn(a, b):
    return jnp.dot(a, b, preferred_element_type=F32)


def dot_nt(a, b):
    return lax.dot_general(a, b, (((1,), (1,)), ((), ())), preferred_element_type=F32)


def pack_stat(lse):
    hi = lse.astype(BF16).astype(F32)
    mid = (lse - hi).astype(BF16).astype(F32)
    low = lse - hi - mid
    shape = (lse.shape[0], 128)
    lane = lax.broadcasted_iota(jnp.int32, shape, 1)
    terms = jnp.where(lane == 0, hi, jnp.where(lane == 1, mid, jnp.where(lane == 2, low, 0.0)))
    return terms.astype(BF16)


def unpack_stat(tile):
    return jnp.sum(tile.astype(F32), axis=-1, keepdims=True)


def kernel(
    len_ref, draft_ref, q_ref, cache_ref, vup_ref, proj_ref, out_ref,
    kbuf, qf, qsib, qbuf, res, psib, mbuf, rbuf, latb, wbuf, vbuf, hvall, pbuf, fbuf,
    k_sem, qp_sem, qs_sem, qr_sem, ff_sem, ps_sem, pr_sem, ms_sem, mr_sem,
    ws_sem, wr_sem, vs_sem, vr_sem, hs_sem, hr_sem, fs_sem, fr_sem,
):
    ctx = lax.axis_index("ctx")
    z = lax.axis_index("grp")
    core = lax.rem(ctx, 2)
    chip = lax.div(ctx, 2)
    x = lax.div(chip, 4)
    y = lax.rem(chip, 4)
    sib = ctx + 1 - 2 * core
    head = core * 4 + z

    def remote(src, dst, send, recv, to_ctx, to_z=None):
        where = {"ctx": to_ctx} if to_z is None else {"ctx": to_ctx, "grp": to_z}
        return pltpu.make_async_remote_copy(
            src_ref=src, dst_ref=dst, send_sem=send, recv_sem=recv,
            device_id=where, device_id_type=MESH,
        )

    def arrived(ref, sem):
        remote(ref, ref, sem, sem, sib).wait_recv()

    def left(ref, sem):
        remote(ref, ref, sem, sem, sib).wait_send()

    plane = [(dx, dy) for dx in range(4) for dy in range(4) if dx or dy]
    column = [(dc, dz) for dz in range(4) for dc in range(2) if dc or dz]

    def cache_copy(r):
        return pltpu.make_async_copy(cache_ref.at[r], kbuf.at[r], k_sem.at[r])

    for r in range(REQ_DEV):
        both = [q_ref[r, s].astype(F32) for s in range(2)]
        qf[r] = jnp.concatenate(both, axis=0)
    theirs = pl.ds((1 - core) * OWN, OWN)
    pair_q = remote(qf.at[theirs], qsib, qp_sem.at[0], qp_sem.at[1], sib)
    pair_q.start()
    for i in range(REQ_DEV):
        cache_copy((i % 2) * OWN + i // 2).start()
    pair_q.wait_recv()
    for rr in range(OWN):
        r = core * OWN + rr
        mine, other = qf[r], qsib[rr]
        first = jnp.where(core == 0, mine, other)
        second = jnp.where(core == 0, other, mine)
        qbuf[r, chip] = jnp.concatenate([first, second], axis=0).astype(BF16)
        for dx, dy in plane:
            to = lax.rem(x + dx, 4) * 4 + lax.rem(y + dy, 4)
            remote(
                qbuf.at[r, chip], qbuf.at[r, chip], qs_sem.at[rr], qr_sem.at[r], 2 * to + core
            ).start()

    rows = pl.ds(pl.multiple_of(head * 128, 128), 128)

    def cut(cc, zz):
        return proj_ref.at[:, pl.ds(pl.multiple_of(zz * 2 * COLS + cc * COLS, 128), COLS)]

    pltpu.make_async_copy(cut(core, z), wbuf.at[rows], wr_sem).start()
    pltpu.make_async_copy(vup_ref.at[0], vbuf.at[head], vr_sem).start()
    for dc, dz in column:
        cc, zz = lax.rem(core + dc, 2), lax.rem(z + dz, 4)
        remote(vup_ref.at[0], vbuf.at[head], vs_sem, vr_sem, 2 * chip + cc, zz).start()
        remote(cut(cc, zz), wbuf.at[rows], ws_sem, wr_sem, 2 * chip + cc, zz).start()

    def forward(rr):
        r = core * OWN + rr
        arrived(qbuf.at[r, pl.ds(0, CHIPS - 1)], qr_sem.at[r])
        remote(qbuf.at[r], qbuf.at[r], ff_sem.at[0, r], ff_sem.at[1, r], sib).start()

    def attend(r):
        cache_copy(r).wait()
        first_pos = ctx * KEYS
        pos = first_pos + lax.broadcasted_iota(jnp.int32, (8, KEYS), 1)
        draft = lax.div(lax.broadcasted_iota(jnp.int32, (8, KEYS), 0), 4)
        seen = (pos < len_ref[r]) | (pos == draft_ref[r, 0])
        seen = seen | ((pos == draft_ref[r, 1]) & (draft == 1))
        bias = jnp.where(seen, 0.0, NEG_FILL)
        queries = qbuf[r].reshape(CHIPS * ROWS, WIDTH)
        scores = dot_nn(queries, kbuf[r])
        scores = (scores.reshape(32, 8, KEYS) * SCALE + bias[None]).reshape(CHIPS * ROWS, KEYS)
        top = jnp.max(scores, axis=1, keepdims=True)
        weights = jnp.exp2(scores - top)
        total = jnp.sum(weights, axis=1, keepdims=True)
        numer = dot_nt(weights.astype(BF16), kbuf[r, :LAT, :])
        numer = (numer * (1.0 / total)).astype(BF16)
        stat = pack_stat(top + jnp.log2(total))
        for h in range(2):
            res[r, h, :, :LAT] = numer[h * HALF:(h + 1) * HALF]
            res[r, h, :, LAT:] = stat[h * HALF:(h + 1) * HALF]
        remote(res.at[r, 1 - core], psib.at[r], ps_sem.at[r], pr_sem.at[r], sib).start()

    def block_to(r, i):
        to = 8 * core + lax.rem(i + chip, 8)
        owner = lax.div(r, OWN)
        rr = lax.rem(r, OWN)
        dest = 2 * to + owner
        src, dst = mbuf.at[r, lax.rem(i + chip, 8)], rbuf.at[rr, chip]
        return dest, src, dst, rr

    def merge(r):
        arrived(psib.at[r], pr_sem.at[r])
        a, b = res[r, core], psib[r]
        la, lb = unpack_stat(a[:, LAT:]), unpack_stat(b[:, LAT:])
        top = jnp.maximum(la, lb)
        wa, wb = jnp.exp2(la - top), jnp.exp2(lb - top)
        both = wa + wb
        inv = 1.0 / both
        merged = a[:, :LAT].astype(F32) * (wa * inv) + b[:, :LAT].astype(F32) * (wb * inv)
        stat = pack_stat(top + jnp.log2(both))
        mbuf[r, :, :, :LAT] = merged.astype(BF16).reshape(8, ROWS, LAT)
        mbuf[r, :, :, LAT:] = stat.reshape(8, ROWS, 128)

        def send(i, carry):
            dest, src, dst, rr = block_to(r, i)

            @pl.when(dest == ctx)
            def _():
                pltpu.make_async_copy(src, dst, mr_sem.at[rr]).start()

            @pl.when(dest != ctx)
            def _():
                remote(src, dst, ms_sem.at[r, i], mr_sem.at[rr], dest).start()

            return carry

        lax.fori_loop(0, 8, send, 0)

    forward(0)

    def step(j, carry):
        @pl.when(core == 1)
        def _():
            arrived(qbuf.at[j], ff_sem.at[1, j])

        attend(j)

        @pl.when(j > 0)
        def _():
            merge(j + OWN - 1)

        @pl.when(j < OWN - 1)
        def _():
            forward(j + 1)

        @pl.when(core == 0)
        def _():
            arrived(qbuf.at[j + OWN], ff_sem.at[1, j + OWN])

        attend(j + OWN)
        merge(j)
        return carry

    lax.fori_loop(0, OWN, step, 0)
    merge(REQ_DEV - 1)

    def finish(rr, carry):
        arrived(rbuf.at[rr], mr_sem.at[rr])
        parts = rbuf[rr]
        lse = unpack_stat(parts[:, :, LAT:])
        top = jnp.max(lse, axis=0, keepdims=True)
        w = jnp.exp2(lse - top)
        w = w * (1.0 / jnp.sum(w, axis=0, keepdims=True))
        latb[rr] = jnp.sum(parts[:, :, :LAT].astype(F32) * w, axis=0).astype(BF16)
        return carry

    lax.fori_loop(0, OWN, finish, 0)

    arrived(vbuf, vr_sem)
    latent = latb[...].reshape(OWN * ROWS, LAT)
    row = lax.broadcasted_iota(jnp.int32, (16, OWN * ROWS), 1)
    at = lax.broadcasted_iota(jnp.int32, (16, OWN * ROWS), 0)
    place = (core * OWN + row // 16) * 2 + (row // 4) % 2
    row_head = ((row // 8) % 2) * 4 + row % 4
    own_slot = z * 2 + core
    for h in range(8):
        values = dot_nn(latent, vbuf[h]).astype(BF16)
        pick = jnp.where((place == at) & (row_head == h), 1.0, 0.0).astype(BF16)
        hvall[own_slot, :, h * 128:(h + 1) * 128] = dot_nn(pick, values).astype(BF16)
    for dc, dz in column:
        cc, zz = lax.rem(core + dc, 2), lax.rem(z + dz, 4)
        remote(
            hvall.at[own_slot], hvall.at[own_slot], hs_sem, hr_sem, 2 * chip + cc, zz
        ).start()
    arrived(wbuf, wr_sem)
    arrived(hvall.at[pl.ds(0, 7)], hr_sem)

    acts = jnp.concatenate(
        [(hvall[2 * g].astype(F32) + hvall[2 * g + 1].astype(F32)).astype(BF16) for g in range(4)],
        axis=0,
    )
    partial = dot_nn(acts, wbuf[...])
    for jj in range(4):
        piece = partial[:, jj * OUT:(jj + 1) * OUT]
        piece = jnp.concatenate([piece, jnp.zeros((64, 256 - OUT), F32)], axis=1)
        pbuf[jj] = piece.astype(BF16).reshape(4, 16, 256)

    def out_to(jj, dz):
        zz = lax.rem(z + dz, 4)
        dest = z * 8 + core * 4 + jj
        return dest, zz, (dest == ctx) & (zz == z)

    for dz in range(4):
        for jj in range(4):
            dest, zz, here = out_to(jj, dz)

            @pl.when(here)
            def _():
                pltpu.make_async_copy(pbuf.at[jj, zz], fbuf.at[chip], fr_sem).start()

            @pl.when(jnp.logical_not(here))
            def _():
                remote(
                    pbuf.at[jj, zz], fbuf.at[chip], fs_sem.at[jj, dz], fr_sem, dest, zz
                ).start()

    arrived(fbuf, fr_sem)
    out_ref[...] = jnp.sum(fbuf[...].astype(F32), axis=0)[:, :OUT].astype(BF16)

    pair_q.wait_send()
    for rr in range(OWN):
        r = core * OWN + rr
        left(qbuf.at[r, pl.ds(0, CHIPS - 1)], qs_sem.at[rr])
        left(qbuf.at[r], ff_sem.at[0, r])
    left(vbuf.at[pl.ds(0, 7)], vs_sem)
    left(wbuf.at[pl.ds(0, 7 * 128)], ws_sem)
    left(hvall.at[pl.ds(0, 7)], hs_sem)

    def gone(r, carry):
        left(psib.at[r], ps_sem.at[r])

        def one(i, inner):
            dest, src, dst, rr = block_to(r, i)

            @pl.when(dest != ctx)
            def _():
                left(src, ms_sem.at[r, i])

            return inner

        return lax.fori_loop(0, 8, one, carry)

    lax.fori_loop(0, REQ_DEV, gone, 0)
    for dz in range(4):
        for jj in range(4):
            dest, zz, here = out_to(jj, dz)

            @pl.when(jnp.logical_not(here))
            def _():
                left(pbuf.at[jj, zz], fs_sem.at[jj, dz])


def local(query, latent_cache, context_lengths, draft_positions, value_up, out_proj):
    dma = pltpu.SemaphoreType.DMA
    vmem = pltpu.VMEM
    flat = pl.pallas_call(
        kernel,
        out_shape=jax.ShapeDtypeStruct((16, OUT), BF16),
        in_specs=[
            pl.BlockSpec(memory_space=pltpu.SMEM),
            pl.BlockSpec(memory_space=pltpu.SMEM),
            pl.BlockSpec(memory_space=pltpu.VMEM),
            pl.BlockSpec(memory_space=pl.ANY),
            pl.BlockSpec(memory_space=pl.ANY),
            pl.BlockSpec(memory_space=pl.ANY),
        ],
        out_specs=pl.BlockSpec(memory_space=pltpu.VMEM),
        scratch_shapes=[
            vmem((REQ_DEV, WIDTH, KEYS), BF16),
            vmem((REQ_DEV, 8, WIDTH), F32),
            vmem((OWN, 8, WIDTH), F32),
            vmem((REQ_DEV, CHIPS, ROWS, WIDTH), BF16),
            vmem((REQ_DEV, 2, HALF, STAT), BF16),
            vmem((REQ_DEV, HALF, STAT), BF16),
            vmem((REQ_DEV, 8, ROWS, STAT), BF16),
            vmem((OWN, CHIPS, ROWS, STAT), BF16),
            vmem((OWN, ROWS, LAT), BF16),
            vmem((8 * 128, COLS), BF16),
            vmem((8, LAT, 128), BF16),
            vmem((8, 16, 8 * 128), BF16),
            vmem((4, 4, 16, 256), BF16),
            vmem((CHIPS, 16, 256), BF16),
            dma((REQ_DEV,)), dma((2,)), dma((OWN,)), dma((REQ_DEV,)), dma((2, REQ_DEV)),
            dma((REQ_DEV,)), dma((REQ_DEV,)), dma((REQ_DEV, 8)), dma((OWN,)),
            dma, dma, dma, dma, dma, dma, dma((4, 4)), dma,
        ],
        compiler_params=pltpu.CompilerParams(
            has_side_effects=True, vmem_limit_bytes=56 * 2**20
        ),
        name="latent_decode",
    )(context_lengths, draft_positions, query, jnp.swapaxes(latent_cache, 1, 2), value_up, out_proj)
    return flat.reshape(REQ_DEV, 2, OUT)


def solution(mesh):
    return jax.shard_map(
        local,
        mesh=mesh,
        in_specs=(
            P("grp", None, "ctx", None),
            P("grp", "ctx", None),
            P("grp"),
            P("grp", None),
            P(("ctx", "grp"), None, None),
            P(("ctx", "grp"), None),
        ),
        out_specs=P("grp", None, "ctx"),
        check_vma=False,
    )
```

```python
import math

import jax
import jax.numpy as jnp
from jax import lax
from jax.experimental import pallas as pl
from jax.experimental.pallas import tpu as pltpu
from jax.sharding import PartitionSpec as P

LAT = 512
ROPE = 64
NOPE = 128
WIDTH = LAT + ROPE
STAT = LAT + 128

YARN_GAIN = (0.1 * math.log(40.0) + 1.0) ** 2
SCALE = (NOPE + ROPE) ** -0.5 * YARN_GAIN * math.log2(math.e)
NEG_FILL = -1e30

REQ_DEV = 8
OWN = REQ_DEV // 2
KEYS = 2048
CHIPS = 16
ROWS = 16
HALF = 8 * ROWS
COLS = 896
OUT = 224
F32 = jnp.float32
BF16 = jnp.bfloat16
MESH = pl.DeviceIdType.MESH


def dot_nn(a, b):
    return jnp.dot(a, b, preferred_element_type=F32)


def dot_nt(a, b):
    return lax.dot_general(a, b, (((1,), (1,)), ((), ())), preferred_element_type=F32)


def pack_stat(lse):
    hi = lse.astype(BF16).astype(F32)
    mid = (lse - hi).astype(BF16).astype(F32)
    low = lse - hi - mid
    shape = (lse.shape[0], 128)
    lane = lax.broadcasted_iota(jnp.int32, shape, 1)
    terms = jnp.where(lane == 0, hi, jnp.where(lane == 1, mid, jnp.where(lane == 2, low, 0.0)))
    return terms.astype(BF16)


def unpack_stat(tile):
    return jnp.sum(tile.astype(F32), axis=-1, keepdims=True)


def kernel(
    len_ref, draft_ref, q_ref, cache_ref, vup_ref, proj_ref, out_ref,
    kbuf, qf, qsib, qbuf, res, psib, mbuf, ubuf, vout, rbuf, lbuf, latb, wbuf, vbuf, hvall, pbuf, fbuf,
    k_sem, qp_sem, q1s_sem, q1r_sem, q2s_sem, q2r_sem, ff_sem, ps_sem, pr_sem,
    us_sem, ur_sem, ns_sem, nr_sem, ls_sem, lr_sem, ws_sem, wr_sem, vs_sem, vr_sem, hs_sem, hr_sem, fs_sem, fr_sem,
):
    ctx = lax.axis_index("ctx")
    z = lax.axis_index("grp")
    core = lax.rem(ctx, 2)
    chip = lax.div(ctx, 2)
    x = lax.div(chip, 4)
    y = lax.rem(chip, 4)
    sib = ctx + 1 - 2 * core
    head = core * 4 + z

    def remote(src, dst, send, recv, to_ctx, to_z=None):
        where = {"ctx": to_ctx} if to_z is None else {"ctx": to_ctx, "grp": to_z}
        return pltpu.make_async_remote_copy(
            src_ref=src, dst_ref=dst, send_sem=send, recv_sem=recv,
            device_id=where, device_id_type=MESH,
        )

    def arrived(ref, sem):
        remote(ref, ref, sem, sem, sib).wait_recv()

    def left(ref, sem):
        remote(ref, ref, sem, sem, sib).wait_send()

    def turned(rr):
        odd = lax.rem(rr, 2)
        return x + odd * (y - x), y + odd * (x - y), odd

    def chip_at(u, v, odd):
        return (u * 4 + v) + odd * 3 * (v - u)

    column = [(dc, dz) for dz in range(4) for dc in range(2) if dc or dz]

    def cache_copy(r):
        return pltpu.make_async_copy(cache_ref.at[r], kbuf.at[r], k_sem.at[r])

    gate = pltpu.get_barrier_semaphore()
    plane = [(dx, dy) for dx in range(4) for dy in range(4) if dx or dy]
    near = [(sib, z)]
    for d in range(1, 4):
        for dc in range(2):
            near.append((2 * chip + lax.rem(core + dc, 2), lax.rem(z + d, 4)))
    for dx, dy in plane:
        near.append((2 * (lax.rem(x + dx, 4) * 4 + lax.rem(y + dy, 4)) + core, z))
    for to_ctx, to_z in near:
        pl.semaphore_signal(
            gate, inc=1, device_id={"ctx": to_ctx, "grp": to_z}, device_id_type=MESH
        )
    for i in range(REQ_DEV):
        cache_copy((i % 2) * OWN + i // 2).start()

    for r in range(REQ_DEV):
        both = [q_ref[r, s].astype(F32) for s in range(2)]
        qf[r] = jnp.concatenate(both, axis=0)
    pl.semaphore_wait(gate, len(near))
    theirs = pl.ds((1 - core) * OWN, OWN)
    pair_q = remote(qf.at[theirs], qsib, qp_sem.at[0], qp_sem.at[1], sib)
    pair_q.start()
    pair_q.wait_recv()
    for rr in range(OWN):
        r = core * OWN + rr
        mine, other = qf[r], qsib[rr]
        first = jnp.where(core == 0, mine, other)
        second = jnp.where(core == 0, other, mine)
        u, v, odd = turned(rr)
        slot = u * 4 + v
        qbuf[r, slot] = jnp.concatenate([first, second], axis=0).astype(BF16)
        if rr == 0:
            for dx, dy in plane:
                to = lax.rem(x + dx, 4) * 4 + lax.rem(y + dy, 4)
                remote(
                    qbuf.at[r, slot], qbuf.at[r, slot], q2s_sem.at[rr], q2r_sem.at[rr],
                    2 * to + core,
                ).start()
            continue
        for d in range(1, 4):
            to = chip_at(u, lax.rem(v + d, 4), odd)
            remote(
                qbuf.at[r, slot], qbuf.at[r, slot], q1s_sem.at[rr], q1r_sem.at[rr], 2 * to + core
            ).start()

    rows = pl.ds(pl.multiple_of(head * 128, 128), 128)

    def column_group(cc, zz):
        return lax.rem(x + 4 + zz - 2 * zz * cc, 4) * 2 + lax.rem(cc + y, 2)

    def cut(cc, zz):
        return proj_ref.at[:, pl.ds(pl.multiple_of(column_group(cc, zz) * COLS, 128), COLS)]

    pltpu.make_async_copy(cut(core, z), wbuf.at[rows], wr_sem).start()
    pltpu.make_async_copy(vup_ref.at[0], vbuf.at[head], vr_sem).start()
    for dc, dz in column:
        cc, zz = lax.rem(core + dc, 2), lax.rem(z + dz, 4)
        remote(vup_ref.at[0], vbuf.at[head], vs_sem, vr_sem, 2 * chip + cc, zz).start()
        remote(cut(cc, zz), wbuf.at[rows], ws_sem, wr_sem, 2 * chip + cc, zz).start()

    def spread(rr):
        r = core * OWN + rr
        u, v, odd = turned(rr)
        arrived(qbuf.at[r, pl.ds(0, 3)], q1r_sem.at[rr])
        line = qbuf.at[r, pl.ds(4 * u, 4)]
        for d in range(1, 4):
            to = chip_at(lax.rem(u + d, 4), v, odd)
            remote(line, line, q2s_sem.at[rr], q2r_sem.at[rr], 2 * to + core).start()

    def forward(rr, count):
        r = core * OWN + rr
        arrived(qbuf.at[r, pl.ds(0, count)], q2r_sem.at[rr])
        remote(qbuf.at[r], qbuf.at[r], ff_sem.at[0, r], ff_sem.at[1, r], sib).start()

    def attend(r):
        cache_copy(r).wait()
        first_pos = ctx * KEYS
        pos = first_pos + lax.broadcasted_iota(jnp.int32, (8, KEYS), 1)
        draft = lax.div(lax.broadcasted_iota(jnp.int32, (8, KEYS), 0), 4)
        seen = (pos < len_ref[r]) | (pos == draft_ref[0, r])
        seen = seen | ((pos == draft_ref[1, r]) & (draft == 1))
        bias = jnp.where(seen, 0.0, NEG_FILL)
        queries = qbuf[r].reshape(CHIPS * ROWS, WIDTH)
        scores = dot_nn(queries, kbuf[r])
        scores = (scores.reshape(32, 8, KEYS) * SCALE + bias[None]).reshape(CHIPS * ROWS, KEYS)
        top = jnp.max(scores, axis=1, keepdims=True)
        weights = jnp.exp2(scores - top)
        total = jnp.sum(weights, axis=1, keepdims=True)
        numer = dot_nt(weights.astype(BF16), kbuf[r, :LAT, :])
        numer = (numer * (1.0 / total)).astype(BF16)
        stat = pack_stat(top + jnp.log2(total))
        for h in range(2):
            res[r, h, :, :LAT] = numer[h * HALF:(h + 1) * HALF]
            res[r, h, :, LAT:] = stat[h * HALF:(h + 1) * HALF]
        remote(res.at[r, 1 - core], psib.at[r], ps_sem.at[r], pr_sem.at[r], sib).start()

    def line_to(r, i):
        owner, rr = lax.div(r, OWN), lax.rem(r, OWN)
        u, v, odd = turned(rr)
        dest = 2 * chip_at(2 * core + i, v, odd) + owner
        return dest, mbuf.at[r, i], ubuf.at[rr, u], rr

    def merge(r):
        arrived(psib.at[r], pr_sem.at[r])
        a, b = res[r, core], psib[r]
        la, lb = unpack_stat(a[:, LAT:]), unpack_stat(b[:, LAT:])
        top = jnp.maximum(la, lb)
        wa, wb = jnp.exp2(la - top), jnp.exp2(lb - top)
        both = wa + wb
        inv = 1.0 / both
        merged = a[:, :LAT].astype(F32) * (wa * inv) + b[:, :LAT].astype(F32) * (wb * inv)
        stat = pack_stat(top + jnp.log2(both))
        mbuf[r, :, :, :, :LAT] = merged.astype(BF16).reshape(2, 4, ROWS, LAT)
        mbuf[r, :, :, :, LAT:] = stat.reshape(2, 4, ROWS, 128)

    def send_line(r):
        for i in range(2):
            dest, src, dst, rr = line_to(r, i)

            @pl.when(dest == ctx)
            def _():
                pltpu.make_async_copy(src, dst, ur_sem.at[rr]).start()

            @pl.when(dest != ctx)
            def _():
                remote(src, dst, us_sem.at[r, i], ur_sem.at[rr], dest).start()

    def block_to(r, i):
        owner = lax.div(r, OWN)
        u, v, odd = turned(OWN - 1)
        t = lax.rem(i + 2 * v + u, 8)
        to_u, to_v = 2 * core + lax.div(t, 4), lax.rem(t, 4)
        dest = 2 * chip_at(to_u, to_v, odd) + owner
        return dest, mbuf.at[r, lax.div(t, 4), to_v], lbuf.at[chip]

    def send_blocks(r):
        def one(i, carry):
            dest, src, dst = block_to(r, i)

            @pl.when(dest == ctx)
            def _():
                pltpu.make_async_copy(src, dst, lr_sem).start()

            @pl.when(dest != ctx)
            def _():
                remote(src, dst, ls_sem.at[lax.div(r, OWN), i], lr_sem, dest).start()

            return carry

        lax.fori_loop(0, 8, one, 0)

    def joined(parts):
        lse = unpack_stat(parts[:, :, LAT:])
        top = jnp.max(lse, axis=0, keepdims=True)
        w = jnp.exp2(lse - top)
        total = jnp.sum(w, axis=0, keepdims=True)
        w = w * (1.0 / total)
        latent = jnp.sum(parts[:, :, :LAT].astype(F32) * w, axis=0)
        return latent, (top + jnp.log2(total))[0]

    def fold(rr):
        u, v, odd = turned(rr)
        arrived(ubuf.at[rr], ur_sem.at[rr])
        latent, lse = joined(ubuf[rr].reshape(4, 4 * ROWS, STAT))
        vout[rr, :, :, :LAT] = latent.astype(BF16).reshape(4, ROWS, LAT)
        vout[rr, :, :, LAT:] = pack_stat(lse).reshape(4, ROWS, 128)
        rbuf[rr, v] = vout[rr, v]
        for d in range(1, 4):
            to_v = lax.rem(v + d, 4)
            dest = 2 * chip_at(u, to_v, odd) + core
            remote(vout.at[rr, to_v], rbuf.at[rr, v], ns_sem.at[rr], nr_sem.at[rr], dest).start()

    for rr in range(1, OWN):
        spread(rr)
    forward(0, CHIPS - 1)

    def step(j, carry):
        @pl.when(core == 1)
        def _():
            arrived(qbuf.at[j], ff_sem.at[1, j])

        attend(j)

        @pl.when(j > 0)
        def _():
            merge(j + OWN - 1)
            send_line(j + OWN - 1)

        @pl.when(j < OWN - 1)
        def _():
            forward(j + 1, 12)

        @pl.when(core == 0)
        def _():
            arrived(qbuf.at[j + OWN], ff_sem.at[1, j + OWN])

        attend(j + OWN)
        merge(j)

        @pl.when(j < OWN - 1)
        def _():
            send_line(j)

        @pl.when(j == OWN - 1)
        def _():
            send_blocks(j)

        @pl.when(j >= 2)
        def _():
            fold(j - 2)

        return carry

    lax.fori_loop(0, OWN, step, 0)
    merge(REQ_DEV - 1)
    send_blocks(REQ_DEV - 1)
    fold(OWN - 2)

    def finish(rr, carry):
        arrived(rbuf.at[rr, pl.ds(0, 3)], nr_sem.at[rr])
        latent, lse = joined(rbuf[rr])
        latb[rr] = latent.astype(BF16)
        return carry

    lax.fori_loop(0, OWN - 1, finish, 0)
    arrived(lbuf, lr_sem)
    latb[OWN - 1] = joined(lbuf[...])[0].astype(BF16)

    arrived(vbuf, vr_sem)
    latent = latb[...].reshape(OWN * ROWS, LAT)
    row = lax.broadcasted_iota(jnp.int32, (16, OWN * ROWS), 1)
    at = lax.broadcasted_iota(jnp.int32, (16, OWN * ROWS), 0)
    place = ((row // 8) % 2) * 8 + (row // 16) * 2 + (row // 4) % 2
    own_slot = z * 2 + core
    for hz in range(4):
        found = jnp.zeros((16, 128), F32)
        for cc in range(2):
            values = dot_nn(latent, vbuf[cc * 4 + hz]).astype(BF16)
            keep = (place == at) & (row % 4 == hz) & ((row // 8) % 2 == cc)
            found += dot_nn(jnp.where(keep, 1.0, 0.0).astype(BF16), values)
        hvall[own_slot, :, hz * 128:(hz + 1) * 128] = found.astype(BF16)
    for dc, dz in column:
        cc, zz = lax.rem(core + dc, 2), lax.rem(z + dz, 4)
        remote(
            hvall.at[own_slot], hvall.at[own_slot], hs_sem, hr_sem, 2 * chip + cc, zz
        ).start()
    arrived(wbuf, wr_sem)
    arrived(hvall.at[pl.ds(0, 7)], hr_sem)

    def group_acts(g):
        a, b = hvall[2 * g].astype(F32), hvall[2 * g + 1].astype(F32)
        left = jnp.concatenate([a[:8], b[:8]], axis=0)
        right = jnp.concatenate([a[8:], b[8:]], axis=0)
        return jnp.concatenate([left, right], axis=1)

    acts = jnp.concatenate([group_acts(g) for g in range(4)], axis=0).astype(BF16)
    partial = dot_nn(acts, wbuf[...])
    for jj in range(4):
        piece = partial[:, jj * OUT:(jj + 1) * OUT]
        piece = jnp.concatenate([piece, jnp.zeros((64, 256 - OUT), F32)], axis=1)
        pbuf[jj] = piece.astype(BF16).reshape(4, 16, 256)

    def out_to(jj, dz):
        zz = lax.rem(z + dz, 4)
        dest = column_group(core, z) * 4 + jj
        return dest, zz, (dest == ctx) & (zz == z)

    for dz in range(4):
        for jj in range(4):
            dest, zz, here = out_to(jj, dz)

            @pl.when(here)
            def _():
                pltpu.make_async_copy(pbuf.at[jj, zz], fbuf.at[chip], fr_sem).start()

            @pl.when(jnp.logical_not(here))
            def _():
                remote(
                    pbuf.at[jj, zz], fbuf.at[chip], fs_sem.at[jj, dz], fr_sem, dest, zz
                ).start()

    arrived(fbuf, fr_sem)
    result = jnp.sum(fbuf[...].astype(F32), axis=0)[:, :OUT]
    for r in range(REQ_DEV):
        out_ref[r] = result[2 * r:2 * r + 2].astype(BF16)

    pair_q.wait_send()
    for rr in range(OWN):
        r = core * OWN + rr
        left(qbuf.at[r], ff_sem.at[0, r])
        if rr == 0:
            left(qbuf.at[r, pl.ds(0, CHIPS - 1)], q2s_sem.at[rr])
        else:
            left(qbuf.at[r, pl.ds(0, 3)], q1s_sem.at[rr])
            left(qbuf.at[r, pl.ds(0, 12)], q2s_sem.at[rr])
        if rr < OWN - 1:
            left(rbuf.at[rr, pl.ds(0, 3)], ns_sem.at[rr])
    left(vbuf.at[pl.ds(0, 7)], vs_sem)
    left(wbuf.at[pl.ds(0, 7 * 128)], ws_sem)
    left(hvall.at[pl.ds(0, 7)], hs_sem)

    def gone(r, carry):
        left(psib.at[r], ps_sem.at[r])

        @pl.when(lax.rem(r, OWN) < OWN - 1)
        def _():
            for i in range(2):
                dest, src, dst, rr = line_to(r, i)

                @pl.when(dest != ctx)
                def _():
                    left(src, us_sem.at[r, i])

        @pl.when(lax.rem(r, OWN) == OWN - 1)
        def _():
            for i in range(8):
                dest, src, dst = block_to(r, i)

                @pl.when(dest != ctx)
                def _():
                    left(src, ls_sem.at[lax.div(r, OWN), i])

        return carry

    lax.fori_loop(0, REQ_DEV, gone, 0)
    for dz in range(4):
        for jj in range(4):
            dest, zz, here = out_to(jj, dz)

            @pl.when(jnp.logical_not(here))
            def _():
                left(pbuf.at[jj, zz], fs_sem.at[jj, dz])


def local(query, latent_cache, context_lengths, draft_positions, value_up, out_proj):
    dma = pltpu.SemaphoreType.DMA
    vmem = pltpu.VMEM
    return pl.pallas_call(
        kernel,
        out_shape=jax.ShapeDtypeStruct((REQ_DEV, 2, OUT), BF16),
        in_specs=[
            pl.BlockSpec(memory_space=pltpu.SMEM),
            pl.BlockSpec(memory_space=pltpu.SMEM),
            pl.BlockSpec(memory_space=pltpu.VMEM),
            pl.BlockSpec(memory_space=pl.ANY),
            pl.BlockSpec(memory_space=pl.ANY),
            pl.BlockSpec(memory_space=pl.ANY),
        ],
        out_specs=pl.BlockSpec(memory_space=pltpu.VMEM),
        scratch_shapes=[
            vmem((REQ_DEV, WIDTH, KEYS), BF16),
            vmem((REQ_DEV, 8, WIDTH), F32),
            vmem((OWN, 8, WIDTH), F32),
            vmem((REQ_DEV, CHIPS, ROWS, WIDTH), BF16),
            vmem((REQ_DEV, 2, HALF, STAT), BF16),
            vmem((REQ_DEV, HALF, STAT), BF16),
            vmem((REQ_DEV, 2, 4, ROWS, STAT), BF16),
            vmem((OWN, 4, 4, ROWS, STAT), BF16),
            vmem((OWN, 4, ROWS, STAT), BF16),
            vmem((OWN, 4, ROWS, STAT), BF16),
            vmem((CHIPS, ROWS, STAT), BF16),
            vmem((OWN, ROWS, LAT), BF16),
            vmem((8 * 128, COLS), BF16),
            vmem((8, LAT, 128), BF16),
            vmem((8, 16, 4 * 128), BF16),
            vmem((4, 4, 16, 256), BF16),
            vmem((CHIPS, 16, 256), BF16),
            dma((REQ_DEV,)), dma((2,)), dma((OWN,)), dma((OWN,)), dma((OWN,)), dma((OWN,)),
            dma((2, REQ_DEV)), dma((REQ_DEV,)), dma((REQ_DEV,)),
            dma((REQ_DEV, 2)), dma((OWN,)), dma((OWN,)), dma((OWN,)), dma((2, 8)), dma,
            dma, dma, dma, dma, dma, dma, dma((4, 4)), dma,
        ],
        compiler_params=pltpu.CompilerParams(
            collective_id=0, has_side_effects=True, vmem_limit_bytes=56 * 2**20
        ),
        name="latent_decode",
    )(
        context_lengths, jnp.swapaxes(draft_positions, 0, 1), query,
        jnp.swapaxes(latent_cache, 1, 2), value_up, out_proj,
    )


def solution(mesh):
    return jax.shard_map(
        local,
        mesh=mesh,
        in_specs=(
            P("grp", None, "ctx", None),
            P("grp", "ctx", None),
            P("grp"),
            P("grp", None),
            P(("ctx", "grp"), None, None),
            P(("ctx", "grp"), None),
        ),
        out_specs=P("grp", None, "ctx"),
        check_vma=False,
    )
```

```python
import math

import jax
import jax.numpy as jnp
from jax import lax
from jax.experimental import pallas as pl
from jax.experimental.pallas import tpu as pltpu
from jax.sharding import PartitionSpec as P

LAT = 512
ROPE = 64
NOPE = 128
WIDTH = LAT + ROPE
PADDED = 640
PATHS = (slice(0, 256), slice(256, PADDED))
STAT = LAT + 128

YARN_GAIN = (0.1 * math.log(40.0) + 1.0) ** 2
SCALE = (NOPE + ROPE) ** -0.5 * YARN_GAIN * math.log2(math.e)
NEG_FILL = -1e30

REQ_DEV = 8
OWN = REQ_DEV // 2
KEYS = 2048
CHIPS = 16
ROWS = 16
HALF = 8 * ROWS
COLS = 896
OUT = 224
PART = 512
F32 = jnp.float32
BF16 = jnp.bfloat16
MESH = pl.DeviceIdType.MESH


def dot_nn(a, b):
    return jnp.dot(a, b, preferred_element_type=F32)


def dot_nt(a, b):
    return lax.dot_general(a, b, (((1,), (1,)), ((), ())), preferred_element_type=F32)


def pack_stat(lse):
    hi = lse.astype(BF16).astype(F32)
    mid = (lse - hi).astype(BF16).astype(F32)
    low = lse - hi - mid
    shape = (lse.shape[0], 128)
    lane = lax.broadcasted_iota(jnp.int32, shape, 1)
    terms = jnp.where(lane == 0, hi, jnp.where(lane == 1, mid, jnp.where(lane == 2, low, 0.0)))
    return terms.astype(BF16)


def unpack_stat(tile):
    return jnp.sum(tile.astype(F32), axis=-1, keepdims=True)


def kernel(
    len_ref, draft_ref, q_ref, cache_ref, vup_ref, proj_ref, out_ref,
    kbuf, store_a, store_b, qf, qsib, qbuf, res, psib, mbuf, ubuf, vout, rbuf, lbuf, latb, wbuf, vbuf, hvall, sort, pbuf, fbuf,
    k_sem, qp_sem, q1s_sem, q1r_sem, q2s_sem, q2r_sem, ff_sem, ps_sem, pr_sem,
    us_sem, ur_sem, ns_sem, nr_sem, ls_sem, lr_sem, ws_sem, wr_sem, vs_sem, vr_sem, vf_sem, hs_sem, hr_sem, fs_sem, fr_sem,
):
    ctx = lax.axis_index("ctx")
    z = lax.axis_index("grp")
    core = lax.rem(ctx, 2)
    chip = lax.div(ctx, 2)
    x = lax.div(chip, 4)
    y = lax.rem(chip, 4)
    sib = ctx + 1 - 2 * core
    head = core * 4 + z

    def remote(src, dst, send, recv, to_ctx, to_z=None):
        where = {"ctx": to_ctx} if to_z is None else {"ctx": to_ctx, "grp": to_z}
        return pltpu.make_async_remote_copy(
            src_ref=src, dst_ref=dst, send_sem=send, recv_sem=recv,
            device_id=where, device_id_type=MESH,
        )

    def arrived(ref, sem):
        remote(ref, ref, sem, sem, sib).wait_recv()

    def left(ref, sem):
        remote(ref, ref, sem, sem, sib).wait_send()

    def turned(rr, owner):
        odd = lax.rem(rr + owner, 2)
        return x + odd * (y - x), y + odd * (x - y), odd

    def chip_at(u, v, odd):
        return (u * 4 + v) + odd * 3 * (v - u)

    column = [(dc, dz) for dz in range(4) for dc in range(2) if dc or dz]

    def cache_copy(r):
        return pltpu.make_async_copy(cache_ref.at[r], kbuf.at[r], k_sem.at[r])

    gate = pltpu.get_barrier_semaphore()
    plane = [(dx, dy) for dx in range(4) for dy in range(4) if dx or dy]
    near = [(sib, z)]
    for d in range(1, 4):
        for dc in range(2):
            near.append((2 * chip + lax.rem(core + dc, 2), lax.rem(z + d, 4)))
    for dx, dy in plane:
        near.append((2 * (lax.rem(x + dx, 4) * 4 + lax.rem(y + dy, 4)) + core, z))
    for to_ctx, to_z in near:
        pl.semaphore_signal(
            gate, inc=1, device_id={"ctx": to_ctx, "grp": to_z}, device_id_type=MESH
        )
    for i in range(REQ_DEV):
        cache_copy((lax.rem(core + i, 2)) * OWN + i // 2).start()

    def lanes_of(rr, along_y):
        return PATHS[(rr + along_y) % 2]

    for r in range(REQ_DEV):
        both = [q_ref[r, s].astype(F32) for s in range(2)]
        qf[r] = jnp.concatenate(both, axis=0)
    pl.semaphore_wait(gate, len(near))
    theirs = pl.ds((1 - core) * OWN, OWN)
    pair_q = remote(qf.at[theirs], qsib, qp_sem.at[0], qp_sem.at[1], sib)
    pair_q.start()
    rows = pl.ds(pl.multiple_of(head * 128, 128), 128)

    def column_group(cc, zz):
        return lax.rem(x + zz + 2 * cc, 4) * 2 + lax.rem(cc + y, 2)

    def cut(cc, zz):
        return proj_ref.at[:, pl.ds(pl.multiple_of(column_group(cc, zz) * COLS, 128), COLS)]

    pltpu.make_async_copy(vup_ref.at[0], vbuf.at[head], vr_sem).start()
    for dz in range(1, 4):
        remote(vup_ref.at[0], vbuf.at[head], vs_sem, vr_sem, ctx, lax.rem(z + dz, 4)).start()
    pltpu.make_async_copy(cut(core, z), wbuf.at[rows], wr_sem).start()
    for dc, dz in column:
        cc, zz = lax.rem(core + dc, 2), lax.rem(z + dz, 4)
        remote(cut(cc, zz), wbuf.at[rows], ws_sem, wr_sem, 2 * chip + cc, zz).start()

    def share_values():
        mine = vbuf.at[pl.ds(core * 4, 4)]
        arrived(mine, vr_sem)
        remote(mine, mine, vf_sem.at[0], vf_sem.at[1], sib).start()

    pair_q.wait_recv()
    for rr in range(OWN):
        r = core * OWN + rr
        mine, other = qf[r], qsib[rr]
        first = jnp.where(core == 0, mine, other)
        second = jnp.where(core == 0, other, mine)
        block = jnp.concatenate([first, second], axis=0)
        block = jnp.concatenate([block, jnp.zeros((ROWS, PADDED - WIDTH), F32)], axis=1)
        qbuf[r, x, y] = block.astype(BF16)
        for along_y in range(2):
            mine = qbuf.at[r, x, y, :, lanes_of(rr, along_y)]
            for d in range(1, 4):
                to = x * 4 + lax.rem(y + d, 4) if along_y else lax.rem(x + d, 4) * 4 + y
                remote(
                    mine, mine, q1s_sem.at[rr, along_y], q1r_sem.at[rr, along_y], 2 * to + core
                ).start()

    at = lax.broadcasted_iota(jnp.int32, (512, 512), 0)
    row = lax.broadcasted_iota(jnp.int32, (512, 512), 1)
    origin = (at % 64) // 2 * 16 + at // 256 * 8 + at % 2 * 4 + at // 64 % 4
    sort[...] = jnp.where(origin == row, 1.0, 0.0).astype(BF16)

    def spread(rr):
        r = core * OWN + rr
        for along_y in range(2):
            lanes = lanes_of(rr, along_y)
            arrived(qbuf.at[r, 0, pl.ds(0, 3), :, lanes], q1r_sem.at[rr, along_y])
            line = qbuf.at[r, x, :, :, lanes] if along_y else qbuf.at[r, :, y, :, lanes]
            for d in range(1, 4):
                to = lax.rem(x + d, 4) * 4 + y if along_y else x * 4 + lax.rem(y + d, 4)
                remote(
                    line, line, q2s_sem.at[rr, along_y], q2r_sem.at[rr, along_y], 2 * to + core
                ).start()

    def forward(rr):
        r = core * OWN + rr
        for along_y in range(2):
            lanes = lanes_of(rr, along_y)
            arrived(qbuf.at[r, pl.ds(0, 3), :, :, lanes], q2r_sem.at[rr, along_y])
        remote(qbuf.at[r], qbuf.at[r], ff_sem.at[0, r], ff_sem.at[1, r], sib).start()

    def score(r, store, part):
        odd = lax.rem(r + lax.div(r, OWN), 2)
        keys = slice(part * PART, (part + 1) * PART)
        first_pos = ctx * KEYS + part * PART
        pos = first_pos + lax.broadcasted_iota(jnp.int32, (8, PART), 1)
        draft = lax.div(lax.broadcasted_iota(jnp.int32, (8, PART), 0), 4)
        seen = (pos < len_ref[r]) | (pos == draft_ref[0, r])
        seen = seen | ((pos == draft_ref[1, r]) & (draft == 1))
        bias = jnp.where(seen, 0.0, NEG_FILL)
        queries = jnp.concatenate(
            [
                qbuf[r, k // 4 + odd * (k % 4 - k // 4), k % 4 + odd * (k // 4 - k % 4)]
                for k in range(CHIPS)
            ],
            axis=0,
        )
        scores = dot_nn(queries[:, :WIDTH], kbuf[r, :, keys])
        scores = (scores.reshape(32, 8, PART) * SCALE + bias[None]).reshape(CHIPS * ROWS, PART)
        store[:, keys] = scores
        return jnp.max(scores, axis=1, keepdims=True)

    def attend(r, store, top, ahead=None):
        total, numer, next_top = 0.0, 0.0, None
        for part in range(KEYS // PART):
            if ahead is not None:
                part_top = score(*ahead, part)
                next_top = part_top if next_top is None else jnp.maximum(next_top, part_top)
            keys = slice(part * PART, (part + 1) * PART)
            weights = jnp.exp2(store[:, keys] - top)
            total += jnp.sum(weights, axis=1, keepdims=True)
            numer += dot_nt(weights.astype(BF16), kbuf[r, :LAT, keys])
        numer = (numer * (1.0 / total)).astype(BF16)
        stat = pack_stat(top + jnp.log2(total))
        for h in range(2):
            res[r, h, :, :LAT] = numer[h * HALF:(h + 1) * HALF]
            res[r, h, :, LAT:] = stat[h * HALF:(h + 1) * HALF]
        remote(res.at[r, 1 - core], psib.at[r], ps_sem.at[r], pr_sem.at[r], sib).start()
        return next_top

    def line_to(r, i):
        owner, rr = lax.div(r, OWN), lax.rem(r, OWN)
        u, v, odd = turned(rr, owner)
        dest = 2 * chip_at(2 * core + i, v, odd) + owner
        return dest, mbuf.at[r, i], ubuf.at[rr, u], rr

    def merge(r):
        arrived(psib.at[r], pr_sem.at[r])
        a, b = res[r, core], psib[r]
        la, lb = unpack_stat(a[:, LAT:]), unpack_stat(b[:, LAT:])
        top = jnp.maximum(la, lb)
        wa, wb = jnp.exp2(la - top), jnp.exp2(lb - top)
        both = wa + wb
        inv = 1.0 / both
        merged = a[:, :LAT].astype(F32) * (wa * inv) + b[:, :LAT].astype(F32) * (wb * inv)
        stat = pack_stat(top + jnp.log2(both))
        mbuf[r, :, :, :, :LAT] = merged.astype(BF16).reshape(2, 4, ROWS, LAT)
        mbuf[r, :, :, :, LAT:] = stat.reshape(2, 4, ROWS, 128)

    def send_line(r):
        for i in range(2):
            dest, src, dst, rr = line_to(r, i)

            @pl.when(dest == ctx)
            def _():
                pltpu.make_async_copy(src, dst, ur_sem.at[rr]).start()

            @pl.when(dest != ctx)
            def _():
                remote(src, dst, us_sem.at[r, i], ur_sem.at[rr], dest).start()

    def block_to(r, i):
        owner = lax.div(r, OWN)
        u, v, odd = turned(OWN - 1, owner)
        t = lax.rem(i + 2 * v + u, 8)
        to_u, to_v = 2 * core + lax.div(t, 4), lax.rem(t, 4)
        dest = 2 * chip_at(to_u, to_v, odd) + owner
        return dest, mbuf.at[r, lax.div(t, 4), to_v], lbuf.at[chip]

    def send_blocks(r):
        def one(i, carry):
            dest, src, dst = block_to(r, i)

            @pl.when(dest == ctx)
            def _():
                pltpu.make_async_copy(src, dst, lr_sem).start()

            @pl.when(dest != ctx)
            def _():
                remote(src, dst, ls_sem.at[lax.div(r, OWN), i], lr_sem, dest).start()

            return carry

        lax.fori_loop(0, 8, one, 0)

    def joined(parts):
        lse = unpack_stat(parts[:, :, LAT:])
        top = jnp.max(lse, axis=0, keepdims=True)
        w = jnp.exp2(lse - top)
        total = jnp.sum(w, axis=0, keepdims=True)
        w = w * (1.0 / total)
        latent = jnp.sum(parts[:, :, :LAT].astype(F32) * w, axis=0)
        return latent, (top + jnp.log2(total))[0]

    def fold(rr):
        u, v, odd = turned(rr, core)
        arrived(ubuf.at[rr], ur_sem.at[rr])
        latent, lse = joined(ubuf[rr].reshape(4, 4 * ROWS, STAT))
        vout[rr, :, :, :LAT] = latent.astype(BF16).reshape(4, ROWS, LAT)
        vout[rr, :, :, LAT:] = pack_stat(lse).reshape(4, ROWS, 128)
        rbuf[rr, v] = vout[rr, v]
        for d in range(1, 4):
            to_v = lax.rem(v + d, 4)
            dest = 2 * chip_at(u, to_v, odd) + core
            remote(vout.at[rr, to_v], rbuf.at[rr, v], ns_sem.at[rr], nr_sem.at[rr], dest).start()

    def own(rr):
        return core * OWN + rr

    def other(rr):
        return (1 - core) * OWN + rr

    def came(rr):
        arrived(qbuf.at[other(rr)], ff_sem.at[1, other(rr)])
        cache_copy(other(rr)).wait()

    def merge_pair(rr):
        for owner in range(2):
            merge(owner * OWN + rr)
            send_line(owner * OWN + rr)

    spread(0)
    spread(1)
    forward(0)
    spread(2)
    cache_copy(own(0)).wait()
    top = score(own(0), store_a, 0)
    for part in range(1, KEYS // PART):
        top = jnp.maximum(top, score(own(0), store_a, part))

    def step(j, top):
        came(j)
        top = attend(own(j), store_a, top, (other(j), store_b))

        @pl.when(j > 0)
        def _():
            merge_pair(j - 1)

        @pl.when(j == 0)
        def _():
            spread(3)

        for rr in range(1, OWN):

            @pl.when(j == rr - 1)
            def _():
                forward(rr)

        cache_copy(own(j + 1)).wait()
        top = attend(other(j), store_b, top, (own(j + 1), store_a))

        @pl.when(j == OWN - 2)
        def _():
            share_values()
            fold(0)

        return top

    top = lax.fori_loop(0, OWN - 1, step, top)
    came(OWN - 1)
    top = attend(own(OWN - 1), store_a, top, (other(OWN - 1), store_b))
    merge_pair(OWN - 2)
    attend(other(OWN - 1), store_b, top)
    fold(1)
    for owner in range(2):
        merge(owner * OWN + OWN - 1)
        send_blocks(owner * OWN + OWN - 1)
    fold(OWN - 2)

    def settle():
        pair_q.wait_send()
        for rr in range(OWN):
            r = core * OWN + rr
            left(qbuf.at[r], ff_sem.at[0, r])
            for along_y in range(2):
                lanes = lanes_of(rr, along_y)
                left(qbuf.at[r, 0, pl.ds(0, 3), :, lanes], q1s_sem.at[rr, along_y])
                left(qbuf.at[r, pl.ds(0, 3), :, :, lanes], q2s_sem.at[rr, along_y])
            if rr < OWN - 1:
                left(rbuf.at[rr, pl.ds(0, 3)], ns_sem.at[rr])
        left(vbuf.at[pl.ds(0, 3)], vs_sem)
        left(vbuf.at[pl.ds(0, 4)], vf_sem.at[0])
        left(wbuf.at[pl.ds(0, 7 * 128)], ws_sem)

        def gone(r, carry):
            left(psib.at[r], ps_sem.at[r])

            @pl.when(lax.rem(r, OWN) < OWN - 1)
            def _():
                for i in range(2):
                    dest, src, dst, rr = line_to(r, i)

                    @pl.when(dest != ctx)
                    def _():
                        left(src, us_sem.at[r, i])

            @pl.when(lax.rem(r, OWN) == OWN - 1)
            def _():
                for i in range(8):
                    dest, src, dst = block_to(r, i)

                    @pl.when(dest != ctx)
                    def _():
                        left(src, ls_sem.at[lax.div(r, OWN), i])

            return carry

        lax.fori_loop(0, REQ_DEV, gone, 0)

    def finish(rr, carry):
        arrived(rbuf.at[rr, pl.ds(0, 3)], nr_sem.at[rr])
        latent, lse = joined(rbuf[rr])
        latb[rr] = latent.astype(BF16)
        return carry

    lax.fori_loop(0, OWN - 1, finish, 0)

    arrived(vbuf.at[pl.ds(4 - 4 * core, 4)], vf_sem.at[1])
    own_slot = z * 2 + core

    def head_values(start, count, which):
        latent = latb[pl.ds(start, count)].reshape(count * ROWS, LAT)
        row = lax.broadcasted_iota(jnp.int32, (count * ROWS, 128), 0)
        row_head = row // 8 % 2 * 4 + row % 4
        found = jnp.zeros((count * ROWS, 128), F32)
        for h in range(8):
            found = jnp.where(row_head == h, dot_nn(latent, vbuf[h]), found)
        part = hvall.at[own_slot, pl.ds(start, count)]
        part[...] = found.astype(BF16).reshape(count, ROWS, 128)
        for dc, dz in column:
            cc, zz = lax.rem(core + dc, 2), lax.rem(z + dz, 4)
            remote(
                part, part, hs_sem.at[which], hr_sem.at[which], 2 * chip + cc, zz
            ).start()

    head_values(0, OWN - 1, 0)
    arrived(lbuf, lr_sem)
    latb[OWN - 1] = joined(lbuf[...])[0].astype(BF16)
    head_values(OWN - 1, 1, 1)
    arrived(wbuf, wr_sem)
    settle()
    arrived(hvall.at[pl.ds(0, 7), pl.ds(0, OWN - 1)], hr_sem.at[0])
    arrived(hvall.at[pl.ds(0, 7), pl.ds(0, 1)], hr_sem.at[1])

    sorted_values = dot_nn(sort[...], hvall[...].reshape(512, 128)).astype(BF16)
    acts = jnp.concatenate([sorted_values[h * 64:(h + 1) * 64] for h in range(8)], axis=1)
    partial = dot_nn(acts, wbuf[...])
    for jj in range(4):
        piece = partial[:, jj * OUT:(jj + 1) * OUT]
        piece = jnp.concatenate([piece, jnp.zeros((64, 256 - OUT), F32)], axis=1)
        pbuf[jj] = piece.astype(BF16).reshape(4, 16, 256)

    def out_to(jj, dz):
        zz = lax.rem(z + dz, 4)
        dest = column_group(core, z) * 4 + jj
        return dest, zz, (dest == ctx) & (zz == z)

    for dz in range(4):
        for jj in range(4):
            dest, zz, here = out_to(jj, dz)

            @pl.when(here)
            def _():
                pltpu.make_async_copy(pbuf.at[jj, zz], fbuf.at[chip], fr_sem).start()

            @pl.when(jnp.logical_not(here))
            def _():
                remote(
                    pbuf.at[jj, zz], fbuf.at[chip], fs_sem.at[jj, dz], fr_sem, dest, zz
                ).start()

    arrived(fbuf, fr_sem)
    result = jnp.sum(fbuf[...].astype(F32), axis=0)[:, :OUT]
    for r in range(REQ_DEV):
        out_ref[r] = result[2 * r:2 * r + 2].astype(BF16)

    for dz in range(4):
        for jj in range(4):
            dest, zz, here = out_to(jj, dz)

            @pl.when(jnp.logical_not(here))
            def _():
                left(pbuf.at[jj, zz], fs_sem.at[jj, dz])

    left(hvall.at[pl.ds(0, 7), pl.ds(0, OWN - 1)], hs_sem.at[0])
    left(hvall.at[pl.ds(0, 7), pl.ds(0, 1)], hs_sem.at[1])


def local(query, latent_cache, context_lengths, draft_positions, value_up, out_proj):
    dma = pltpu.SemaphoreType.DMA
    vmem = pltpu.VMEM
    return pl.pallas_call(
        kernel,
        out_shape=pltpu.VMEM((REQ_DEV, 2, OUT), BF16),
        in_specs=[
            pl.BlockSpec(memory_space=pltpu.SMEM),
            pl.BlockSpec(memory_space=pltpu.SMEM),
            pl.BlockSpec(memory_space=pltpu.VMEM),
            pl.BlockSpec(memory_space=pl.ANY),
            pl.BlockSpec(memory_space=pl.ANY),
            pl.BlockSpec(memory_space=pl.ANY),
        ],
        out_specs=pl.BlockSpec(memory_space=pltpu.VMEM),
        scratch_shapes=[
            vmem((REQ_DEV, WIDTH, KEYS), BF16),
            vmem((CHIPS * ROWS, KEYS), F32),
            vmem((CHIPS * ROWS, KEYS), F32),
            vmem((REQ_DEV, 8, WIDTH), F32),
            vmem((OWN, 8, WIDTH), F32),
            vmem((REQ_DEV, 4, 4, ROWS, PADDED), BF16),
            vmem((REQ_DEV, 2, HALF, STAT), BF16),
            vmem((REQ_DEV, HALF, STAT), BF16),
            vmem((REQ_DEV, 2, 4, ROWS, STAT), BF16),
            vmem((OWN, 4, 4, ROWS, STAT), BF16),
            vmem((OWN, 4, ROWS, STAT), BF16),
            vmem((OWN, 4, ROWS, STAT), BF16),
            vmem((CHIPS, ROWS, STAT), BF16),
            vmem((OWN, ROWS, LAT), BF16),
            vmem((8 * 128, COLS), BF16),
            vmem((8, LAT, 128), BF16),
            vmem((8, OWN, ROWS, 128), BF16),
            vmem((512, 512), BF16),
            vmem((4, 4, 16, 256), BF16),
            vmem((CHIPS, 16, 256), BF16),
            dma((REQ_DEV,)), dma((2,)), dma((OWN, 2)), dma((OWN, 2)), dma((OWN, 2)), dma((OWN, 2)),
            dma((2, REQ_DEV)), dma((REQ_DEV,)), dma((REQ_DEV,)),
            dma((REQ_DEV, 2)), dma((OWN,)), dma((OWN,)), dma((OWN,)), dma((2, 8)), dma,
            dma, dma, dma, dma, dma((2,)), dma((2,)), dma((2,)), dma((4, 4)), dma,
        ],
        compiler_params=pltpu.CompilerParams(
            collective_id=0, has_side_effects=True, vmem_limit_bytes=56 * 2**20
        ),
        name="latent_decode",
    )(
        context_lengths, jnp.swapaxes(draft_positions, 0, 1), query,
        jnp.swapaxes(latent_cache, 1, 2), value_up, out_proj,
    )


def solution(mesh):
    return jax.shard_map(
        local,
        mesh=mesh,
        in_specs=(
            P("grp", None, "ctx", None),
            P("grp", "ctx", None),
            P("grp"),
            P("grp", None),
            P(("ctx", "grp"), None, None),
            P(("ctx", "grp"), None),
        ),
        out_specs=P("grp", None, "ctx"),
        check_vma=False,
    )
```

```python
import functools
import math

import jax
import jax.numpy as jnp
from jax import lax
from jax.experimental import pallas as pl
from jax.experimental.pallas import tpu as pltpu
from jax.sharding import PartitionSpec as P

LAT = 512
ROPE = 64
NOPE = 128
WIDTH = LAT + ROPE
MASKED = WIDTH + 16
PADDED = 640
PATHS = (slice(0, 256), slice(256, PADDED))
STAT = LAT + 128

YARN_GAIN = (0.1 * math.log(40.0) + 1.0) ** 2
SCALE = (NOPE + ROPE) ** -0.5 * YARN_GAIN * math.log2(math.e)
NEG_FILL = -1e30

REQ_DEV = 8
OWN = REQ_DEV // 2
KEYS = 2048
CHIPS = 16
ROWS = 16
HALF = 8 * ROWS
COLS = 896
OUT = 224
PART = 512
F32 = jnp.float32
BF16 = jnp.bfloat16
MESH = pl.DeviceIdType.MESH


def dot_nn(a, b):
    return jnp.dot(a, b, preferred_element_type=F32)


def dot_nt(a, b):
    return lax.dot_general(a, b, (((1,), (1,)), ((), ())), preferred_element_type=F32)


def pack_stat(lse):
    hi = lse.astype(BF16).astype(F32)
    mid = (lse - hi).astype(BF16).astype(F32)
    low = lse - hi - mid
    shape = (lse.shape[0], 128)
    lane = lax.broadcasted_iota(jnp.int32, shape, 1)
    terms = jnp.where(lane == 0, hi, jnp.where(lane == 1, mid, jnp.where(lane == 2, low, 0.0)))
    return terms.astype(BF16)


def unpack_stat(tile):
    return jnp.sum(tile.astype(F32), axis=-1, keepdims=True)


def kernel(
    len_ref, draft_ref, q_ref, cache_ref, vup_ref, proj_ref, out_ref,
    kbuf, store_a, store_b, qf, qin, qbuf, res, psib, mbuf, ubuf, vout, rbuf, lbuf, latb, wbuf, vbuf, hvall, sort, pbuf, fbuf,
    k_sem, q1s_sem, q1r_sem, q2s_sem, q2r_sem, ff_sem, ps_sem, pr_sem,
    us_sem, ur_sem, ns_sem, nr_sem, ls_sem, lr_sem, ws_sem, wr_sem, vs_sem, vr_sem, vf_sem, hs_sem, hr_sem, fs_sem, fr_sem,
):
    ctx = lax.axis_index("ctx")
    z = lax.axis_index("grp")
    core = lax.rem(ctx, 2)
    chip = lax.div(ctx, 2)
    x = lax.div(chip, 4)
    y = lax.rem(chip, 4)
    sib = ctx + 1 - 2 * core
    head = core * 4 + z

    def remote(src, dst, send, recv, to_ctx, to_z=None):
        where = {"ctx": to_ctx} if to_z is None else {"ctx": to_ctx, "grp": to_z}
        return pltpu.make_async_remote_copy(
            src_ref=src, dst_ref=dst, send_sem=send, recv_sem=recv,
            device_id=where, device_id_type=MESH,
        )

    def arrived(ref, sem):
        remote(ref, ref, sem, sem, sib).wait_recv()

    def left(ref, sem):
        remote(ref, ref, sem, sem, sib).wait_send()

    def turned(rr, owner):
        odd = lax.rem(rr + owner, 2)
        return x + odd * (y - x), y + odd * (x - y), odd

    def chip_at(u, v, odd):
        return (u * 4 + v) + odd * 3 * (v - u)

    column = [(dc, dz) for dz in range(4) for dc in range(2) if dc or dz]

    def cache_copy(r):
        return pltpu.make_async_copy(
            cache_ref.at[r], kbuf.at[r, pl.ds(0, WIDTH)], k_sem.at[r]
        )

    gate = pltpu.get_barrier_semaphore()
    near = [(sib, z)]
    for d in range(1, 4):
        for dc in range(2):
            cc = lax.rem(core + dc, 2)
            near.append((2 * (lax.rem(x + d, 4) * 4 + y) + cc, z))
            near.append((2 * (x * 4 + lax.rem(y + d, 4)) + cc, z))
            near.append((2 * chip + cc, lax.rem(z + d, 4)))
    for to_ctx, to_z in near:
        pl.semaphore_signal(
            gate, inc=1, device_id={"ctx": to_ctx, "grp": to_z}, device_id_type=MESH
        )
    def own(rr):
        return core * OWN + rr

    def other(rr):
        return (1 - core) * OWN + rr

    order = [own(0), other(0)] + [half * OWN + rr for rr in range(1, OWN) for half in range(2)]
    for r in order:
        cache_copy(r).start()

    pos = ctx * KEYS + lax.broadcasted_iota(jnp.int32, (16, KEYS), 1)
    draft = lax.broadcasted_iota(jnp.int32, (16, KEYS), 0)
    for r in range(REQ_DEV):
        seen = (pos < len_ref[r]) | (pos == draft_ref[0, r])
        seen = seen | ((pos == draft_ref[1, r]) & (draft == 1)) | (draft > 1)
        kbuf[r, WIDTH:, :] = jnp.where(seen, 0.0, NEG_FILL).astype(BF16)

    def lanes_of(rr, along_y):
        return PATHS[(rr + along_y) % 2]

    lane = lax.broadcasted_iota(jnp.int32, (8, PADDED - WIDTH), 1)
    row_draft = lax.broadcasted_iota(jnp.int32, (8, PADDED - WIDTH), 0) // 4
    pick = jnp.where(lane == row_draft, 1.0, 0.0)
    for r in range(REQ_DEV):
        both = [q_ref[r, s].astype(F32) for s in range(2)]
        block = jnp.concatenate([jnp.concatenate(both, axis=0), pick], axis=1)
        qf[r // OWN, r % 2, r % OWN // 2] = block.astype(BF16)
    for along_y in range(2):
        mine = (y if along_y else x) * 2 + core
        for odd in range(2):
            qin[along_y, odd, mine] = qf[core, odd]
    pl.semaphore_wait(gate, len(near))
    for odd in range(2):
        for along_y in range(2):
            lanes = lanes_of(odd, along_y)
            mine = (y if along_y else x) * 2 + core
            dst = qin.at[along_y, odd, mine, :, :, lanes]
            for d in range(4):
                to = x * 4 + lax.rem(y + d, 4) if along_y else lax.rem(x + d, 4) * 4 + y
                for owner in (core, 1 - core) if d else (1 - core,):
                    remote(
                        qf.at[owner, odd, :, :, lanes], dst,
                        q1s_sem.at[odd, along_y], q1r_sem.at[odd, along_y], 2 * to + owner,
                    ).start()

    rows = pl.ds(pl.multiple_of(head * 128, 128), 128)

    def column_group(cc, zz):
        return lax.rem(x + zz + 2 * cc, 4) * 2 + lax.rem(cc + y, 2)

    def cut(cc, zz):
        return proj_ref.at[:, pl.ds(pl.multiple_of(column_group(cc, zz) * COLS, 128), COLS)]

    pltpu.make_async_copy(vup_ref.at[0], vbuf.at[head], vr_sem).start()
    for dz in range(1, 4):
        remote(vup_ref.at[0], vbuf.at[head], vs_sem, vr_sem, ctx, lax.rem(z + dz, 4)).start()
    pltpu.make_async_copy(cut(core, z), wbuf.at[rows], wr_sem).start()
    for dc, dz in column:
        cc, zz = lax.rem(core + dc, 2), lax.rem(z + dz, 4)
        remote(cut(cc, zz), wbuf.at[rows], ws_sem, wr_sem, 2 * chip + cc, zz).start()

    def share_values():
        mine = vbuf.at[pl.ds(core * 4, 4)]
        arrived(mine, vr_sem)
        remote(mine, mine, vf_sem.at[0], vf_sem.at[1], sib).start()

    at = lax.broadcasted_iota(jnp.int32, (512, 512), 0)
    row = lax.broadcasted_iota(jnp.int32, (512, 512), 1)
    origin = (at % 64) // 2 * 16 + at // 256 * 8 + at % 2 * 4 + at // 64 % 4
    sort[...] = jnp.where(origin == row, 1.0, 0.0).astype(BF16)

    def spread(rr):
        r = core * OWN + rr
        for along_y in range(2):
            lanes = lanes_of(rr, along_y)
            if rr < 2:
                arrived(
                    qin.at[along_y, rr, pl.ds(0, 7), :, :, lanes], q1r_sem.at[rr, along_y]
                )
            for k in range(4):
                both = [qin[along_y, rr % 2, 2 * k + c, rr // 2, :, lanes] for c in range(2)]
                block = jnp.concatenate([half.astype(F32) for half in both], axis=0)
                if along_y:
                    qbuf[r, x, k, :, lanes] = block.astype(BF16)
                else:
                    qbuf[r, k, y, :, lanes] = block.astype(BF16)
            line = qbuf.at[r, x, :, :, lanes] if along_y else qbuf.at[r, :, y, :, lanes]
            for d in range(1, 4):
                to = lax.rem(x + d, 4) * 4 + y if along_y else x * 4 + lax.rem(y + d, 4)
                remote(
                    line, line, q2s_sem.at[rr, along_y], q2r_sem.at[rr, along_y], 2 * to + core
                ).start()

    def forward(rr):
        r = core * OWN + rr
        for along_y in range(2):
            lanes = lanes_of(rr, along_y)
            arrived(qbuf.at[r, pl.ds(0, 3), :, :, lanes], q2r_sem.at[rr, along_y])
        remote(qbuf.at[r], qbuf.at[r], ff_sem.at[0, r], ff_sem.at[1, r], sib).start()

    def score(r, store, part):
        odd = lax.rem(r + lax.div(r, OWN), 2)
        keys = slice(part * PART, (part + 1) * PART)
        queries = jnp.concatenate(
            [
                qbuf[r, k // 4 + odd * (k % 4 - k // 4), k % 4 + odd * (k // 4 - k % 4)]
                for k in range(CHIPS)
            ],
            axis=0,
        )
        scores = dot_nn(queries[:, :MASKED], kbuf[r, :, keys])
        store[:, keys] = scores
        return jnp.max(scores, axis=1, keepdims=True)

    def attend(r, store, top, ahead=None, between=None):
        total, numer, next_top = 0.0, 0.0, None
        top = top * SCALE
        for part in range(KEYS // PART):
            if ahead is not None:
                part_top = score(*ahead, part)
                next_top = part_top if next_top is None else jnp.maximum(next_top, part_top)
            keys = slice(part * PART, (part + 1) * PART)
            weights = jnp.exp2(store[:, keys] * SCALE - top)
            total += jnp.sum(weights, axis=1, keepdims=True)
            numer += dot_nt(weights.astype(BF16), kbuf[r, :LAT, keys])
            if part == 2 and between is not None:
                between()
        numer = (numer * (1.0 / total)).astype(BF16)
        stat = pack_stat(top + jnp.log2(total))
        for h in range(2):
            res[r, h, :, :LAT] = numer[h * HALF:(h + 1) * HALF]
            res[r, h, :, LAT:] = stat[h * HALF:(h + 1) * HALF]
        remote(res.at[r, 1 - core], psib.at[r], ps_sem.at[r], pr_sem.at[r], sib).start()
        return next_top

    def line_to(r, i):
        owner, rr = lax.div(r, OWN), lax.rem(r, OWN)
        u, v, odd = turned(rr, owner)
        dest = 2 * chip_at(2 * core + i, v, odd) + owner
        return dest, mbuf.at[r, i], ubuf.at[rr, u], rr

    def merge(r):
        arrived(psib.at[r], pr_sem.at[r])
        a, b = res[r, core], psib[r]
        la, lb = unpack_stat(a[:, LAT:]), unpack_stat(b[:, LAT:])
        top = jnp.maximum(la, lb)
        wa, wb = jnp.exp2(la - top), jnp.exp2(lb - top)
        both = wa + wb
        inv = 1.0 / both
        merged = a[:, :LAT].astype(F32) * (wa * inv) + b[:, :LAT].astype(F32) * (wb * inv)
        stat = pack_stat(top + jnp.log2(both))
        mbuf[r, :, :, :, :LAT] = merged.astype(BF16).reshape(2, 4, ROWS, LAT)
        mbuf[r, :, :, :, LAT:] = stat.reshape(2, 4, ROWS, 128)

    def send_line(r):
        for i in range(2):
            dest, src, dst, rr = line_to(r, i)

            @pl.when(dest == ctx)
            def _():
                pltpu.make_async_copy(src, dst, ur_sem.at[rr]).start()

            @pl.when(dest != ctx)
            def _():
                remote(src, dst, us_sem.at[r, i], ur_sem.at[rr], dest).start()

    def block_to(r, i):
        owner = lax.div(r, OWN)
        u, v, odd = turned(OWN - 1, owner)
        t = lax.rem(i + 2 * v + u, 8)
        to_u, to_v = 2 * core + lax.div(t, 4), lax.rem(t, 4)
        dest = 2 * chip_at(to_u, to_v, odd) + owner
        return dest, mbuf.at[r, lax.div(t, 4), to_v], lbuf.at[chip]

    def send_blocks(r):
        def one(i, carry):
            dest, src, dst = block_to(r, i)

            @pl.when(dest == ctx)
            def _():
                pltpu.make_async_copy(src, dst, lr_sem).start()

            @pl.when(dest != ctx)
            def _():
                remote(src, dst, ls_sem.at[lax.div(r, OWN), i], lr_sem, dest).start()

            return carry

        lax.fori_loop(0, 8, one, 0)

    def joined(parts):
        lse = unpack_stat(parts[:, :, LAT:])
        top = jnp.max(lse, axis=0, keepdims=True)
        w = jnp.exp2(lse - top)
        total = jnp.sum(w, axis=0, keepdims=True)
        w = w * (1.0 / total)
        latent = jnp.sum(parts[:, :, :LAT].astype(F32) * w, axis=0)
        return latent, (top + jnp.log2(total))[0]

    def fold(rr):
        u, v, odd = turned(rr, core)
        arrived(ubuf.at[rr], ur_sem.at[rr])
        latent, lse = joined(ubuf[rr].reshape(4, 4 * ROWS, STAT))
        vout[rr, :, :, :LAT] = latent.astype(BF16).reshape(4, ROWS, LAT)
        vout[rr, :, :, LAT:] = pack_stat(lse).reshape(4, ROWS, 128)
        rbuf[rr, v] = vout[rr, v]
        for d in range(1, 4):
            to_v = lax.rem(v + d, 4)
            dest = 2 * chip_at(u, to_v, odd) + core
            remote(vout.at[rr, to_v], rbuf.at[rr, v], ns_sem.at[rr], nr_sem.at[rr], dest).start()

    def came(at):
        for owner in range(2):

            @pl.when((core != owner) & (lax.div(order[at], OWN) == owner))
            def _():
                arrived(qbuf.at[order[at]], ff_sem.at[1, order[at]])

        cache_copy(order[at]).wait()

    def before(at):
        return (order[0], order[1]) if at == 2 else (order[at - 1],) if at > 2 else ()

    def merge_before(at):
        for r in before(at):
            merge(r)

    spread(0)
    spread(1)
    forward(0)
    spread(2)
    cache_copy(order[0]).wait()
    top = score(order[0], store_a, 0)
    for part in range(1, KEYS // PART):
        top = jnp.maximum(top, score(order[0], store_a, part))
    forward(1)
    stores = (store_a, store_b)
    for at in range(REQ_DEV - 1):
        came(at + 1)
        top = attend(
            order[at], stores[at % 2], top, (order[at + 1], stores[1 - at % 2]),
            functools.partial(merge_before, at),
        )
        for r in before(at):
            send_line(r)
        if at == 0:
            spread(3)
        if at in (1, 3):
            forward(at // 2 + 2)
        if at == 3:
            share_values()
        if at == 5:
            fold(0)
        if at == 6:
            fold(1)
    attend(order[REQ_DEV - 1], stores[1], top)
    merge(order[REQ_DEV - 2])
    send_blocks(order[REQ_DEV - 2])
    merge(order[REQ_DEV - 1])
    send_blocks(order[REQ_DEV - 1])
    fold(OWN - 2)

    def settle():
        for rr in range(OWN):
            r = core * OWN + rr
            left(qbuf.at[r], ff_sem.at[0, r])
            for along_y in range(2):
                lanes = lanes_of(rr, along_y)
                if rr < 2:
                    left(
                        qin.at[along_y, rr, pl.ds(0, 7), :, :, lanes], q1s_sem.at[rr, along_y]
                    )
                left(qbuf.at[r, pl.ds(0, 3), :, :, lanes], q2s_sem.at[rr, along_y])
            if rr < OWN - 1:
                left(rbuf.at[rr, pl.ds(0, 3)], ns_sem.at[rr])
        left(vbuf.at[pl.ds(0, 3)], vs_sem)
        left(vbuf.at[pl.ds(0, 4)], vf_sem.at[0])
        left(wbuf.at[pl.ds(0, 7 * 128)], ws_sem)

        def gone(r, carry):
            left(psib.at[r], ps_sem.at[r])

            @pl.when(lax.rem(r, OWN) < OWN - 1)
            def _():
                for i in range(2):
                    dest, src, dst, rr = line_to(r, i)

                    @pl.when(dest != ctx)
                    def _():
                        left(src, us_sem.at[r, i])

            @pl.when(lax.rem(r, OWN) == OWN - 1)
            def _():
                for i in range(8):
                    dest, src, dst = block_to(r, i)

                    @pl.when(dest != ctx)
                    def _():
                        left(src, ls_sem.at[lax.div(r, OWN), i])

            return carry

        lax.fori_loop(0, REQ_DEV, gone, 0)

    def finish(rr, carry):
        arrived(rbuf.at[rr, pl.ds(0, 3)], nr_sem.at[rr])
        latent, lse = joined(rbuf[rr])
        latb[rr] = latent.astype(BF16)
        return carry

    lax.fori_loop(0, OWN - 1, finish, 0)

    arrived(vbuf.at[pl.ds(4 - 4 * core, 4)], vf_sem.at[1])
    own_slot = z * 2 + core

    def head_values(start, count, which):
        latent = latb[pl.ds(start, count)].reshape(count * ROWS, LAT)
        row = lax.broadcasted_iota(jnp.int32, (count * ROWS, 128), 0)
        row_head = row // 8 % 2 * 4 + row % 4
        found = jnp.zeros((count * ROWS, 128), F32)
        for h in range(8):
            found = jnp.where(row_head == h, dot_nn(latent, vbuf[h]), found)
        part = hvall.at[own_slot, pl.ds(start, count)]
        part[...] = found.astype(BF16).reshape(count, ROWS, 128)
        for dc, dz in column:
            cc, zz = lax.rem(core + dc, 2), lax.rem(z + dz, 4)
            remote(
                part, part, hs_sem.at[which], hr_sem.at[which], 2 * chip + cc, zz
            ).start()

    head_values(0, OWN - 1, 0)
    arrived(lbuf, lr_sem)
    latb[OWN - 1] = joined(lbuf[...])[0].astype(BF16)
    head_values(OWN - 1, 1, 1)
    arrived(wbuf, wr_sem)
    settle()
    arrived(hvall.at[pl.ds(0, 7), pl.ds(0, OWN - 1)], hr_sem.at[0])
    arrived(hvall.at[pl.ds(0, 7), pl.ds(0, 1)], hr_sem.at[1])

    sorted_values = dot_nn(sort[...], hvall[...].reshape(512, 128)).astype(BF16)
    acts = jnp.concatenate([sorted_values[h * 64:(h + 1) * 64] for h in range(8)], axis=1)
    partial = dot_nn(acts, wbuf[...])
    for jj in range(4):
        piece = partial[:, jj * OUT:(jj + 1) * OUT]
        piece = jnp.concatenate([piece, jnp.zeros((64, 256 - OUT), F32)], axis=1)
        pbuf[jj] = piece.astype(BF16).reshape(4, 16, 256)

    def out_to(jj, dz):
        zz = lax.rem(z + dz, 4)
        dest = column_group(core, z) * 4 + jj
        return dest, zz, (dest == ctx) & (zz == z)

    for dz in range(4):
        for jj in range(4):
            dest, zz, here = out_to(jj, dz)

            @pl.when(here)
            def _():
                pltpu.make_async_copy(pbuf.at[jj, zz], fbuf.at[chip], fr_sem).start()

            @pl.when(jnp.logical_not(here))
            def _():
                remote(
                    pbuf.at[jj, zz], fbuf.at[chip], fs_sem.at[jj, dz], fr_sem, dest, zz
                ).start()

    arrived(fbuf, fr_sem)
    result = jnp.sum(fbuf[...].astype(F32), axis=0)[:, :OUT]
    for r in range(REQ_DEV):
        out_ref[r] = result[2 * r:2 * r + 2].astype(BF16)

    for dz in range(4):
        for jj in range(4):
            dest, zz, here = out_to(jj, dz)

            @pl.when(jnp.logical_not(here))
            def _():
                left(pbuf.at[jj, zz], fs_sem.at[jj, dz])

    left(hvall.at[pl.ds(0, 7), pl.ds(0, OWN - 1)], hs_sem.at[0])
    left(hvall.at[pl.ds(0, 7), pl.ds(0, 1)], hs_sem.at[1])


def local(query, latent_cache, context_lengths, draft_positions, value_up, out_proj):
    dma = pltpu.SemaphoreType.DMA
    vmem = pltpu.VMEM
    return pl.pallas_call(
        kernel,
        out_shape=pltpu.VMEM((REQ_DEV, 2, OUT), BF16),
        in_specs=[
            pl.BlockSpec(memory_space=pltpu.SMEM),
            pl.BlockSpec(memory_space=pltpu.SMEM),
            pl.BlockSpec(memory_space=pltpu.VMEM),
            pl.BlockSpec(memory_space=pl.ANY),
            pl.BlockSpec(memory_space=pl.ANY),
            pl.BlockSpec(memory_space=pl.ANY),
        ],
        out_specs=pl.BlockSpec(memory_space=pltpu.VMEM),
        scratch_shapes=[
            vmem((REQ_DEV, MASKED, KEYS), BF16),
            vmem((CHIPS * ROWS, KEYS), F32),
            vmem((CHIPS * ROWS, KEYS), F32),
            vmem((2, 2, OWN // 2, 8, PADDED), BF16),
            vmem((2, 2, 8, OWN // 2, 8, PADDED), BF16),
            vmem((REQ_DEV, 4, 4, ROWS, PADDED), BF16),
            vmem((REQ_DEV, 2, HALF, STAT), BF16),
            vmem((REQ_DEV, HALF, STAT), BF16),
            vmem((REQ_DEV, 2, 4, ROWS, STAT), BF16),
            vmem((OWN, 4, 4, ROWS, STAT), BF16),
            vmem((OWN, 4, ROWS, STAT), BF16),
            vmem((OWN, 4, ROWS, STAT), BF16),
            vmem((CHIPS, ROWS, STAT), BF16),
            vmem((OWN, ROWS, LAT), BF16),
            vmem((8 * 128, COLS), BF16),
            vmem((8, LAT, 128), BF16),
            vmem((8, OWN, ROWS, 128), BF16),
            vmem((512, 512), BF16),
            vmem((4, 4, 16, 256), BF16),
            vmem((CHIPS, 16, 256), BF16),
            dma((REQ_DEV,)), dma((2, 2)), dma((2, 2)), dma((OWN, 2)), dma((OWN, 2)),
            dma((2, REQ_DEV)), dma((REQ_DEV,)), dma((REQ_DEV,)),
            dma((REQ_DEV, 2)), dma((OWN,)), dma((OWN,)), dma((OWN,)), dma((2, 8)), dma,
            dma, dma, dma, dma, dma((2,)), dma((2,)), dma((2,)), dma((4, 4)), dma,
        ],
        compiler_params=pltpu.CompilerParams(
            collective_id=0, has_side_effects=True, vmem_limit_bytes=56 * 2**20
        ),
        name="latent_decode",
    )(
        context_lengths, jnp.swapaxes(draft_positions, 0, 1), query,
        jnp.swapaxes(latent_cache, 1, 2), value_up, out_proj,
    )


def solution(mesh):
    return jax.shard_map(
        local,
        mesh=mesh,
        in_specs=(
            P("grp", None, "ctx", None),
            P("grp", "ctx", None),
            P("grp"),
            P("grp", None),
            P(("ctx", "grp"), None, None),
            P(("ctx", "grp"), None),
        ),
        out_specs=P("grp", None, "ctx"),
        check_vma=False,
    )
```
